32 devices in a mesh: patch: 8 (over z, y), probe: 4 (over x, core).
Axes of the slice: x: 2, y: 2, z: 4, core: 2. Of those that a mesh axis runs over, the one named last changes fastest.
Arguments:
- probe_columns: bfloat16 [16384, 512], P('patch', 'probe'), may hold values from -6 to 6
- near_field: bfloat16 [128, 16, 128, 128], P('patch')
- column_ids: int32 [128, 16], P('patch'), may hold values from 0 to 127, as said below
- block_counts: int32 [128], P('patch'), may hold values from 1 to 16, as said below
- sketch_matrix: bfloat16 [512, 256], replicated, may hold values from -0.25 to 0.25
Outputs:
- sample: bfloat16 [16384, 512], P('patch', 'probe')
- row_basis: float32 [256, 16384], P('probe', 'patch')
The draws below stay inside these ranges and needn't reach their ends.
Inputs may be any that keep to these rules, and one draw needn't show every extreme that they name: column_ids[b, 0] = b; every column_ids[b, n] is a row block of the patch device that owns b or of one of the 2 patch devices before or after it. `block_counts`: the number of live slots differs strongly from patch device to patch device.
All inputs are finite; a program needn't handle non-finite values.
Results may differ from the reference program's by a relative error of at most 0.0032.
Values may be sent and summed in bfloat16 or wider, within the bound.
A program may use at most 64 MiB of HBM per device.

```python
import math
import jax
import jax.numpy as jnp
from jax import lax

BLK = 128
BLK_DEV = 16
NNZ = 16
REACH = 2
PROBES = 512
RANK = 64
BLOCKS = 128
ROWS = 16384
SKETCH = 256
N_PROBE = 4


def draw_near_field(key, part):
    key_entries, key_scales = jax.random.split(jax.random.fold_in(key, 11))
    shape = (BLOCKS, NNZ, BLK, BLK)
    ramp_scale = 0.5 + jnp.arange(BLOCKS, dtype=jnp.float32) / max(BLOCKS - 1, 1)
    entries = jax.random.normal(key_entries, shape, jnp.float32)
    spread = jax.random.uniform(key_scales, (BLOCKS, BLK), jnp.float32, math.log(0.3), math.log(3.0))
    entries = entries / math.sqrt(BLK * NNZ)
    identity_block = jnp.eye(BLK, dtype=jnp.float32)
    first_slot = (jnp.arange(NNZ) == 0).astype(jnp.float32)
    values = entries + 2.0 * first_slot[None, :, None, None] * identity_block[None, None]
    row_scale = ramp_scale[:, None] * jnp.exp(spread)
    return (values * row_scale[:, None, :, None]).astype(jnp.bfloat16)


def draw_column_ids(key, part):
    owner_device = jnp.arange(BLOCKS, dtype=jnp.int32) // BLK_DEV
    devices = BLOCKS // BLK_DEV
    low_block = jnp.maximum(owner_device - REACH, 0) * BLK_DEV
    high_block = jnp.minimum(owner_device + REACH + 1, devices) * BLK_DEV
    column_ids = jax.random.randint(jax.random.fold_in(key, 21), (BLOCKS, NNZ), low_block[:, None], high_block[:, None], dtype=jnp.int32)
    return column_ids.at[:, 0].set(jnp.arange(BLOCKS, dtype=jnp.int32))


def draw_block_counts(key, part):
    key_limit, key_rows = jax.random.split(jax.random.fold_in(key, 31))
    devices = BLOCKS // BLK_DEV
    owner_device = jnp.arange(BLOCKS, dtype=jnp.int32) // BLK_DEV
    device_limit = jax.random.randint(key_limit, (devices,), max(NNZ // 2, 1), NNZ + 1, dtype=jnp.int32)
    raw_draw = jax.random.randint(key_rows, (BLOCKS,), 0, 1 << 20, dtype=jnp.int32)
    counts_drawn = 1 + raw_draw % device_limit[owner_device]
    return counts_drawn.at[0].set(NNZ).at[BLOCKS - 1].set(1)


def block_scale(own_key, shape, cuts, least, high):
    def one(dim, blocks):
        steps = jax.random.uniform(jax.random.fold_in(jax.random.fold_in(own_key, 6), dim), (blocks,), jnp.float32, least / len(cuts), high / len(cuts))
        return jnp.repeat(jnp.exp(steps), shape[dim] // blocks).reshape((-1,) + (1,) * (len(shape) - dim - 1))

    level = one(*cuts[0])
    for cut in cuts[1:]:
        level = level * one(*cut)
    return level


def normal_values(own_key, extent, scale, reach, cuts=(), kind=jnp.bfloat16):
    values = jax.random.normal(own_key, extent, jnp.float32) * scale
    if len(cuts) > 0:
        values = block_scale(own_key, extent, cuts, -0.22, 0.18) * values
    return jnp.clip(values, min=-reach, max=reach).astype(kind)


def setup_inputs(seed: int = 0) -> dict:
    streams_of = jax.random.split(jax.random.key(seed), 6)
    probe_columns = normal_values(streams_of[0], (ROWS, PROBES), 1.0, 6.0, ((0, 8), (1, 4)))
    near_field = draw_near_field(jax.random.fold_in(streams_of[5], 71), 0)
    column_ids = draw_column_ids(jax.random.fold_in(streams_of[5], 71), 0)
    block_counts = draw_block_counts(jax.random.fold_in(streams_of[5], 71), 0)
    sketch_matrix = normal_values(streams_of[4], (PROBES, SKETCH), PROBES ** -0.5, 0.25)
    return dict(probe_columns=probe_columns, near_field=near_field, column_ids=column_ids, block_counts=block_counts, sketch_matrix=sketch_matrix)


def reference(probe_columns, near_field, column_ids, block_counts, sketch_matrix):
    blocks = probe_columns.reshape(BLOCKS, BLK, PROBES)
    groups = BLOCKS // BLK_DEV

    def near_rows(group):
        near_group, block_ids, live_count = group
        picked = blocks[block_ids]
        slots = jnp.arange(NNZ, dtype=jnp.int32)
        live_slots = slots[None, :] < live_count[:, None]
        picked = jnp.where(live_slots[:, :, None, None], picked, jnp.zeros_like(picked))
        return jnp.einsum('bnrc,bncp->brp', near_group.astype(jnp.float32), picked.astype(jnp.float32))
    product = lax.map(near_rows, (near_field.reshape(groups, BLK_DEV, NNZ, BLK, BLK), column_ids.reshape(groups, BLK_DEV, NNZ), block_counts.reshape(groups, BLK_DEV)))
    sample = product.reshape(ROWS, PROBES).astype(jnp.bfloat16)
    sketch = lax.dot_general(sketch_matrix.astype(jnp.float32), sample.astype(jnp.float32), (((0,), (1,)), ((), ())), preferred_element_type=jnp.float32)
    pieces = []
    for index in range(N_PROBE):
        factor = sketch[index * RANK:(index + 1) * RANK]
        gram_total = jnp.dot(factor, factor.T, precision=lax.Precision.HIGHEST)
        lower = jnp.linalg.cholesky(gram_total)
        solved = lax.linalg.triangular_solve(lower, factor, left_side=True, lower=True)
        pieces.append(solved * math.sqrt(ROWS))
    return (sample, jnp.concatenate(pieces, 0))
```

```python
import functools
import math

import jax
import jax.numpy as jnp
from jax import lax
from jax.experimental import pallas as pl
from jax.experimental.pallas import tpu as pltpu
from jax.sharding import PartitionSpec as P

REACH = 2
MESH = pl.DeviceIdType.MESH
F32 = jnp.float32
BF16 = jnp.bfloat16
CHUNKS = 4
NT = (((1,), (1,)), ((), ()))
NN = (((1,), (0,)), ((), ()))
HIGHEST = lax.Precision.HIGHEST


def kernel(
    patches, total_rows, probe, nf, ids, counts, psi, sample_out, basis_out,
    win, nfv, idx, psiv, psit, samp, keep, send, crecv, fac, xsend, xrecv, gsend, grecv, bas,
    hs, hr, ls, nfs, sos, cs, cr, xs, xr, gs, gr, bos,
):
    blk_dev, slots, blk, width = nf.shape[0], nf.shape[1], nf.shape[2], probe.shape[2]
    half = blk_dev // 2
    sketch = psi.shape[1]
    rank = sketch // 4
    per = blk_dev // CHUNKS
    cw = per * blk
    levels = patches.bit_length() - 1

    p = lax.axis_index("patch")
    me = lax.axis_index("probe")
    s = 1 - 2 * (p % 2)
    near = p + s
    ahead = p + 2 * s
    behind = p - 2 * s
    has_ahead = jnp.logical_and(ahead >= 0, ahead < patches)
    has_behind = jnp.logical_and(behind >= 0, behind < patches)
    core = me + 1 - 2 * (me % 2)
    side = me + 2 - 4 * (me // 2)

    def flip(level):
        bit = 2**level
        return p + bit - 2 * bit * ((p // bit) % 2)

    barrier = pltpu.get_barrier_semaphore()

    def greet(where):
        pl.semaphore_signal(barrier, inc=1, device_id=where, device_id_type=MESH)

    greet({"patch": near})
    greet({"probe": core})
    greet({"probe": side})
    for level in range(2, levels):
        greet({"patch": flip(level)})

    @pl.when(has_ahead)
    def _():
        greet({"patch": ahead})

    @pl.when(has_behind)
    def _():
        greet({"patch": behind})

    own_copy = pltpu.make_async_copy(probe, win.at[pl.ds(0, blk_dev)], ls.at[0])
    own_copy.start()
    psi_copy = pltpu.make_async_copy(
        psi.at[pl.ds(pl.multiple_of(me * width, width), width)], psiv, ls.at[1]
    )
    psi_copy.start()

    peers = 3 + max(levels - 2, 0) + has_ahead.astype(jnp.int32) + has_behind.astype(jnp.int32)
    pl.semaphore_wait(barrier, peers)

    def halo(k, src, slot, start, count, target):
        return pltpu.make_async_remote_copy(
            src_ref=src, dst_ref=win.at[pl.ds(slot * blk_dev + start, count)],
            send_sem=hs.at[k], recv_sem=hr.at[k], device_id={"patch": target}, device_id_type=MESH,
        )

    first, second = probe.at[pl.ds(0, half)], probe.at[pl.ds(half, half)]
    near_b = halo(0, second, 1, half, half, near)
    near_a = halo(1, first, 1, 0, half, near)
    behind_a = halo(2, first, 2, 0, half, behind)
    behind_b = halo(3, second, 2, half, half, behind)
    ahead_a = halo(4, first, 3, 0, half, ahead)
    ahead_b = halo(5, second, 3, half, half, ahead)
    relay_a = halo(6, win.at[pl.ds(2 * blk_dev, half)], 4, 0, half, near)
    relay_b = halo(7, win.at[pl.ds(blk_dev + half, half)], 4, half, half, ahead)

    near_b.start()

    @pl.when(has_behind)
    def _():
        behind_a.start()

    @pl.when(has_ahead)
    def _():
        ahead_a.start()

    near_a.start()

    @pl.when(has_behind)
    def _():
        behind_b.start()

    @pl.when(has_ahead)
    def _():
        ahead_b.start()

    nf_copies = []
    for c in range(CHUNKS):
        rows = pl.ds(c * per, per)
        copy = pltpu.make_async_copy(nf.at[rows], nfv.at[rows], nfs.at[c])
        copy.start()
        nf_copies.append(copy)

    zero_block = (2 * REACH + 1) * blk_dev
    win[zero_block] = jnp.zeros((blk, width), BF16)

    @pl.loop(0, blk_dev)
    def _(b):
        live = counts[b]
        for n in range(slots):
            column = ids[b, n]
            turn = (column // blk_dev - p) * s
            slot = jnp.where(turn < 0, turn + 2 * REACH + 1, turn)
            place = slot * blk_dev + column % blk_dev
            idx[b, n] = jnp.where(n < live, place, zero_block)

    psi_copy.wait()
    psit[...] = psiv[...].astype(F32).T.astype(BF16).reshape(4, rank, width)
    other = side + 1 - 2 * (side % 2)
    psiq = jnp.concatenate([psit[me], psit[side], psit[core], psit[other]], 0)

    near_b.wait_recv()

    @pl.when(has_ahead)
    def _():
        relay_b.start()
        behind_a.wait_recv()
        relay_a.start()
        behind_b.wait_recv()

    near_a.wait_recv()

    @pl.when(has_behind)
    def _():
        ahead_a.wait_recv()
        ahead_b.wait_recv()
        relay_a.wait_recv()
        relay_b.wait_recv()

    own_copy.wait()

    def core_copy(c):
        return pltpu.make_async_remote_copy(
            src_ref=send.at[c], dst_ref=crecv.at[c], send_sem=cs.at[c], recv_sem=cr.at[c],
            device_id={"probe": core}, device_id_type=MESH,
        )

    def side_copy(c):
        return pltpu.make_async_remote_copy(
            src_ref=xsend.at[c], dst_ref=xrecv.at[c], send_sem=xs.at[c], recv_sem=xr.at[c],
            device_id={"probe": side}, device_id_type=MESH,
        )

    def pass_on(c):
        core_copy(c).wait_recv()
        both = keep[c] + crecv[c]
        fac[c] = both[:rank]
        xsend[c] = both[rank:].astype(BF16)
        side_copy(c).start()

    sample_copies = []
    for c in range(CHUNKS):
        nf_copies[c].wait()

        @pl.loop(c * per, (c + 1) * per)
        def _(b):
            picked = jnp.concatenate([win[idx[b, n]] for n in range(slots)], 0)
            blocks = jnp.concatenate([nfv[b, n] for n in range(slots)], 1)
            samp[b] = lax.dot_general(blocks, picked, NN, preferred_element_type=F32).astype(BF16)

        rows = pl.ds(c * per, per)
        copy = pltpu.make_async_copy(samp.at[rows], sample_out.at[rows], sos.at[c])
        copy.start()
        sample_copies.append(copy)
        part = lax.dot_general(
            psiq, samp[rows].reshape(cw, width), NT, preferred_element_type=F32
        )
        keep[c] = part[: 2 * rank]
        send[c] = part[2 * rank :]
        core_copy(c).start()
        if c > 0:
            pass_on(c - 1)
    pass_on(CHUNKS - 1)

    gram = jnp.zeros((rank, 2 * rank), F32)
    for c in range(CHUNKS):
        side_copy(c).wait_recv()
        factor = fac[c] + xrecv[c].astype(F32)
        fac[c] = factor
        twice = jnp.concatenate([factor, factor], 0)
        gram += lax.dot_general(factor, twice, NT, precision=HIGHEST, preferred_element_type=F32)

    lane = lax.broadcasted_iota(jnp.int32, (rank // 2, 2 * rank), 1)
    packed = jnp.where(lane < rank, gram[: rank // 2], gram[rank // 2 :])

    def gram_copy(level):
        return pltpu.make_async_remote_copy(
            src_ref=gsend.at[level], dst_ref=grecv.at[level], send_sem=gs.at[level],
            recv_sem=gr.at[level], device_id={"patch": flip(level)}, device_id_type=MESH,
        )

    for level in range(levels):
        gsend[level] = packed
        gram_copy(level).start()
        gram_copy(level).wait_recv()
        packed = packed + grecv[level]

    lane = lax.broadcasted_iota(jnp.int32, (rank, 2 * rank), 1)
    row = lax.broadcasted_iota(jnp.int32, (rank, 2 * rank), 0)
    work = jnp.concatenate([pltpu.roll(packed, rank, 1), packed], 0)
    work = jnp.where(lane < rank, jnp.where(lane == row, 1.0, 0.0), work)
    for j in range(rank - 1):
        column = jnp.broadcast_to(work[:, rank + j : rank + j + 1], work.shape)
        pivot_row = work[j : j + 1, :]
        ratio = pivot_row / column[j : j + 1, :]
        work = jnp.where(row > j, work - column * ratio, work)
    pivots = jnp.sum(jnp.where(lane == row + rank, work, 0.0), axis=1, keepdims=True)
    inverse = work[:, :rank] * (lax.rsqrt(pivots) * math.sqrt(total_rows))

    basis_copies = []
    for c in range(CHUNKS):
        columns = pl.ds(c * cw, cw)
        bas[:, columns] = lax.dot_general(
            inverse, fac[c], NN, precision=HIGHEST, preferred_element_type=F32
        )
        copy = pltpu.make_async_copy(bas.at[:, columns], basis_out.at[:, columns], bos.at[c])
        copy.start()
        basis_copies.append(copy)

    near_b.wait_send()
    near_a.wait_send()

    @pl.when(has_behind)
    def _():
        behind_a.wait_send()
        behind_b.wait_send()

    @pl.when(has_ahead)
    def _():
        ahead_a.wait_send()
        ahead_b.wait_send()
        relay_a.wait_send()
        relay_b.wait_send()

    for c in range(CHUNKS):
        core_copy(c).wait_send()
        side_copy(c).wait_send()
        sample_copies[c].wait()
        basis_copies[c].wait()
    for level in range(levels):
        gram_copy(level).wait_send()


def shards(probe_columns, near_field, column_ids, block_counts, sketch_matrix):
    blk_dev, slots, blk, _ = near_field.shape
    rows, width = probe_columns.shape
    sketch = sketch_matrix.shape[1]
    patches = lax.axis_size("patch")
    rank = sketch // lax.axis_size("probe")
    cw = rows // CHUNKS
    levels = patches.bit_length() - 1
    anywhere = pl.BlockSpec(memory_space=pl.ANY)
    scalars = pl.BlockSpec(memory_space=pltpu.SMEM)
    dma = pltpu.SemaphoreType.DMA
    sample, basis = pl.pallas_call(
        functools.partial(kernel, patches, rows * patches),
        out_shape=[
            jax.ShapeDtypeStruct((blk_dev, blk, width), BF16),
            jax.ShapeDtypeStruct((rank, rows), F32),
        ],
        in_specs=[anywhere, anywhere, scalars, scalars, anywhere],
        out_specs=[anywhere, anywhere],
        scratch_shapes=[
            pltpu.VMEM(((2 * REACH + 1) * blk_dev + 1, blk, width), BF16),
            pltpu.VMEM(near_field.shape, BF16),
            pltpu.SMEM((blk_dev, slots), jnp.int32),
            pltpu.VMEM((width, sketch), BF16),
            pltpu.VMEM((4, rank, width), BF16),
            pltpu.VMEM((blk_dev, blk, width), BF16),
            pltpu.VMEM((CHUNKS, 2 * rank, cw), F32),
            pltpu.VMEM((CHUNKS, 2 * rank, cw), F32),
            pltpu.VMEM((CHUNKS, 2 * rank, cw), F32),
            pltpu.VMEM((CHUNKS, rank, cw), F32),
            pltpu.VMEM((CHUNKS, rank, cw), BF16),
            pltpu.VMEM((CHUNKS, rank, cw), BF16),
            pltpu.VMEM((levels, rank // 2, 2 * rank), F32),
            pltpu.VMEM((levels, rank // 2, 2 * rank), F32),
            pltpu.VMEM((rank, rows), F32),
            dma((8,)), dma((8,)), dma((2,)), dma((CHUNKS,)), dma((CHUNKS,)),
            dma((CHUNKS,)), dma((CHUNKS,)), dma((CHUNKS,)), dma((CHUNKS,)),
            dma((levels,)), dma((levels,)), dma((CHUNKS,)),
        ],
        compiler_params=pltpu.CompilerParams(
            collective_id=0, has_side_effects=True, vmem_limit_bytes=48 * 2**20
        ),
    )(
        probe_columns.reshape(blk_dev, blk, width), near_field, column_ids, block_counts,
        sketch_matrix,
    )
    return (sample.reshape(rows, width), basis)


def solution(mesh):
    placed = (P("patch", "probe"), P("patch", None, None, None), P("patch", None), P("patch"), P())
    return jax.shard_map(
        shards,
        mesh=mesh,
        in_specs=placed,
        out_specs=(P("patch", "probe"), P("probe", "patch")),
        check_vma=False,
    )
```

```python
import functools
import math

import jax
import jax.numpy as jnp
from jax import lax
from jax.experimental import pallas as pl
from jax.experimental.pallas import tpu as pltpu
from jax.sharding import PartitionSpec as P

REACH = 2
MESH = pl.DeviceIdType.MESH
F32 = jnp.float32
BF16 = jnp.bfloat16
CHUNKS = 4
NT = (((1,), (1,)), ((), ()))
NN = (((1,), (0,)), ((), ()))
ROW_TILE = 8


def exchange_plan(patches):
    levels = patches.bit_length() - 1
    return [
        [digit << low for digit in range(1, 2 ** min(3, levels - low))]
        for low in range(0, levels, 3)
    ]


def eliminate(work, rank):
    tile = ROW_TILE
    shape = (tile, work.shape[1])
    tiles = [work[i : i + tile] for i in range(0, rank, tile)]
    row = lax.broadcasted_iota(jnp.int32, shape, 0)
    lane = lax.broadcasted_iota(jnp.int32, shape, 1)
    for t in range(len(tiles)):
        live = range(t, len(tiles))
        columns = [
            {i: jnp.broadcast_to(tiles[i][:, rank + t * tile + k : rank + t * tile + k + 1], shape) for i in live}
            for k in range(tile)
        ]
        for k in range(tile):
            scale = 1.0 / columns[k][t][k : k + 1, :]
            ratio = {i: columns[k][i] * scale for i in live}
            ratio[t] = jnp.where(row > k, ratio[t], 0.0)
            for later in columns[k + 1 :]:
                pivot = later[t][k : k + 1, :]
                for i in live:
                    later[i] = later[i] - ratio[i] * pivot
            pivot = tiles[t][k : k + 1, :]
            for i in live:
                tiles[i] = tiles[i] - ratio[i] * pivot
    diagonal = [
        jnp.sum(jnp.where(lane == row + rank + i * tile, part, 0.0), axis=1, keepdims=True)
        for i, part in enumerate(tiles)
    ]
    return jnp.concatenate(tiles, 0), jnp.concatenate(diagonal, 0)


def kernel(
    patches, total_rows, probe, nf, ids_in, counts_in, psi, sample_out, basis_out,
    win, nfv, ids, counts, idx, psiv, psit, samp, keep, send, crecv, fac, xsend, xrecv, split, gsend, grecv, bas,
    hs, hr, ls, nfs, sos, cs, cr, xs, xr, gs, gr, bos,
):
    blk_dev, slots, blk, width = nf.shape[0], nf.shape[1], nf.shape[2], probe.shape[2]
    half = blk_dev // 2
    sketch = psi.shape[1]
    rank = sketch // 4
    per = blk_dev // CHUNKS
    cw = per * blk
    levels = patches.bit_length() - 1

    p = lax.axis_index("patch")
    me = lax.axis_index("probe")
    s = 1 - 2 * (p % 2)
    near = p + s
    ahead = p + 2 * s
    behind = p - 2 * s
    has_ahead = jnp.logical_and(ahead >= 0, ahead < patches)
    has_behind = jnp.logical_and(behind >= 0, behind < patches)
    core = me + 1 - 2 * (me % 2)
    side = me + 2 - 4 * (me // 2)

    def other_patch(mask):
        place = p
        for bit in (2**level for level in range(levels)):
            if mask & bit:
                place = place + bit - 2 * bit * ((p // bit) % 2)
        return place

    peers = exchange_plan(patches)
    group = peers[0][-1] + 1

    barrier = pltpu.get_barrier_semaphore()

    def greet(where):
        pl.semaphore_signal(barrier, inc=1, device_id=where, device_id_type=MESH)

    ahead_out = jnp.logical_and(has_ahead, ahead // group != p // group)
    behind_out = jnp.logical_and(has_behind, behind // group != p // group)
    greet({"probe": core})
    greet({"probe": side})
    for stage in peers:
        for mask in stage:
            greet({"patch": other_patch(mask)})

    @pl.when(ahead_out)
    def _():
        greet({"patch": ahead})

    @pl.when(behind_out)
    def _():
        greet({"patch": behind})

    own_copy = pltpu.make_async_copy(probe, win.at[pl.ds(0, blk_dev)], ls.at[0])
    own_copy.start()
    psi_copy = pltpu.make_async_copy(
        psi.at[pl.ds(pl.multiple_of(me * width, width), width)], psiv, ls.at[1]
    )
    psi_copy.start()
    ids_copy = pltpu.make_async_copy(ids_in, ids, ls.at[2])
    ids_copy.start()
    counts_copy = pltpu.make_async_copy(counts_in, counts, ls.at[3])
    counts_copy.start()

    greeted = 2 + sum(len(stage) for stage in peers)
    pl.semaphore_wait(barrier, greeted + ahead_out.astype(jnp.int32) + behind_out.astype(jnp.int32))

    def halo(k, src, slot, start, count, target):
        return pltpu.make_async_remote_copy(
            src_ref=src, dst_ref=win.at[pl.ds(slot * blk_dev + start, count)],
            send_sem=hs.at[k], recv_sem=hr.at[k], device_id={"patch": target}, device_id_type=MESH,
        )

    first, second = probe.at[pl.ds(0, half)], probe.at[pl.ds(half, half)]
    near_b = halo(0, second, 1, half, half, near)
    near_a = halo(1, first, 1, 0, half, near)
    behind_a = halo(2, first, 2, 0, half, behind)
    behind_b = halo(3, second, 2, half, half, behind)
    ahead_a = halo(4, first, 3, 0, half, ahead)
    ahead_b = halo(5, second, 3, half, half, ahead)
    relay_a = halo(6, win.at[pl.ds(2 * blk_dev, half)], 4, 0, half, near)
    relay_b = halo(7, win.at[pl.ds(blk_dev + half, half)], 4, half, half, ahead)

    near_b.start()

    @pl.when(has_behind)
    def _():
        behind_a.start()

    @pl.when(has_ahead)
    def _():
        ahead_a.start()

    near_a.start()

    @pl.when(has_behind)
    def _():
        behind_b.start()

    @pl.when(has_ahead)
    def _():
        ahead_b.start()

    nf_copies = []
    for c in range(CHUNKS):
        rows = pl.ds(c * per, per)
        copy = pltpu.make_async_copy(nf.at[rows], nfv.at[rows], nfs.at[c])
        copy.start()
        nf_copies.append(copy)

    zero_block = (2 * REACH + 1) * blk_dev
    win[zero_block] = jnp.zeros((blk, width), BF16)

    ids_copy.wait()
    counts_copy.wait()

    @pl.loop(0, blk_dev)
    def _(b):
        live = counts[b]
        for n in range(slots):
            column = ids[b, n]
            turn = (column // blk_dev - p) * s
            slot = jnp.where(turn < 0, turn + 2 * REACH + 1, turn)
            place = slot * blk_dev + column % blk_dev
            idx[b, n] = jnp.where(n < live, place, zero_block)

    psi_copy.wait()
    psit[...] = psiv[...].astype(F32).T.astype(BF16).reshape(4, rank, width)
    other = side + 1 - 2 * (side % 2)
    psiq = jnp.concatenate([psit[me], psit[side], psit[core], psit[other]], 0)

    near_b.wait_recv()

    @pl.when(has_ahead)
    def _():
        relay_b.start()
        behind_a.wait_recv()
        relay_a.start()
        behind_b.wait_recv()

    near_a.wait_recv()

    @pl.when(has_behind)
    def _():
        ahead_a.wait_recv()
        ahead_b.wait_recv()
        relay_a.wait_recv()
        relay_b.wait_recv()

    own_copy.wait()

    def core_copy(c):
        return pltpu.make_async_remote_copy(
            src_ref=send.at[c], dst_ref=crecv.at[c], send_sem=cs.at[c], recv_sem=cr.at[c],
            device_id={"probe": core}, device_id_type=MESH,
        )

    def side_copy(c):
        return pltpu.make_async_remote_copy(
            src_ref=xsend.at[c], dst_ref=xrecv.at[c], send_sem=xs.at[c], recv_sem=xr.at[c],
            device_id={"probe": side}, device_id_type=MESH,
        )

    def pass_on(c):
        core_copy(c).wait_recv()
        both = keep[c] + crecv[c]
        fac[c] = both[:rank]
        xsend[c] = both[rank:].astype(BF16)
        side_copy(c).start()

    sample_copies = []
    for c in range(CHUNKS):
        nf_copies[c].wait()

        @pl.loop(c * per, (c + 1) * per)
        def _(b):
            picked = jnp.concatenate([win[idx[b, n]] for n in range(slots)], 0)
            blocks = jnp.concatenate([nfv[b, n] for n in range(slots)], 1)
            samp[b] = lax.dot_general(blocks, picked, NN, preferred_element_type=F32).astype(BF16)

        rows = pl.ds(c * per, per)
        copy = pltpu.make_async_copy(samp.at[rows], sample_out.at[rows], sos.at[c])
        copy.start()
        sample_copies.append(copy)
        part = lax.dot_general(
            psiq, samp[rows].reshape(cw, width), NT, preferred_element_type=F32
        )
        keep[c] = part[: 2 * rank]
        send[c] = part[2 * rank :]
        core_copy(c).start()
        if c > 0:
            pass_on(c - 1)
    pass_on(CHUNKS - 1)

    gram = jnp.zeros((rank, 2 * rank), F32)
    for c in range(CHUNKS):
        side_copy(c).wait_recv()
        factor = fac[c] + xrecv[c].astype(F32)
        high = factor.astype(BF16)
        low = (factor - high.astype(F32)).astype(BF16)
        split[c] = jnp.concatenate([high, low, high], 0)
        twice_high = jnp.concatenate([high, high], 0)
        twice_low = jnp.concatenate([low, low], 0)
        both = lax.dot_general(split[c, : 2 * rank], twice_high, NT, preferred_element_type=F32)
        cross = lax.dot_general(high, twice_low, NT, preferred_element_type=F32)
        gram += both[:rank] + (both[rank:] + cross)

    lane = lax.broadcasted_iota(jnp.int32, (rank // 2, 2 * rank), 1)
    packed = jnp.where(lane < rank, gram[: rank // 2], gram[rank // 2 :])

    gram_copies = []
    place = 0
    for number, stage in enumerate(peers):
        gsend[number] = packed
        copies = []
        for mask in stage:
            copy = pltpu.make_async_remote_copy(
                src_ref=gsend.at[number], dst_ref=grecv.at[place], send_sem=gs.at[place],
                recv_sem=gr.at[place], device_id={"patch": other_patch(mask)}, device_id_type=MESH,
            )
            copy.start()
            copies.append((copy, place))
            place += 1
        for copy, slot in copies:
            copy.wait_recv()
            packed = packed + grecv[slot]
        gram_copies += copies

    lane = lax.broadcasted_iota(jnp.int32, (rank, 2 * rank), 1)
    row = lax.broadcasted_iota(jnp.int32, (rank, 2 * rank), 0)
    work = jnp.concatenate([pltpu.roll(packed, rank, 1), packed], 0)
    work = jnp.where(lane < rank, jnp.where(lane == row, 1.0, 0.0), work)
    work, pivots = eliminate(work, rank)
    inverse = work[:, :rank] * (lax.rsqrt(pivots) * math.sqrt(total_rows))
    inverse_high = inverse.astype(BF16)
    inverse_low = (inverse - inverse_high.astype(F32)).astype(BF16)
    inverse = jnp.concatenate([inverse_high, inverse_high, inverse_low], 1)

    basis_copies = []
    for c in range(CHUNKS):
        columns = pl.ds(c * cw, cw)
        bas[:, columns] = lax.dot_general(
            inverse, split[c], NN, preferred_element_type=F32
        )
        copy = pltpu.make_async_copy(bas.at[:, columns], basis_out.at[:, columns], bos.at[c])
        copy.start()
        basis_copies.append(copy)

    near_b.wait_send()
    near_a.wait_send()

    @pl.when(has_behind)
    def _():
        behind_a.wait_send()
        behind_b.wait_send()

    @pl.when(has_ahead)
    def _():
        ahead_a.wait_send()
        ahead_b.wait_send()
        relay_a.wait_send()
        relay_b.wait_send()

    for c in range(CHUNKS):
        core_copy(c).wait_send()
        side_copy(c).wait_send()
        sample_copies[c].wait()
        basis_copies[c].wait()
    for copy, _ in gram_copies:
        copy.wait_send()


def shards(probe_columns, near_field, column_ids, block_counts, sketch_matrix):
    blk_dev, slots, blk, _ = near_field.shape
    rows, width = probe_columns.shape
    sketch = sketch_matrix.shape[1]
    patches = lax.axis_size("patch")
    rank = sketch // lax.axis_size("probe")
    cw = rows // CHUNKS
    plan = exchange_plan(patches)
    sends = sum(len(stage) for stage in plan)
    anywhere = pl.BlockSpec(memory_space=pltpu.HBM)
    dma = pltpu.SemaphoreType.DMA
    sample, basis = pl.pallas_call(
        functools.partial(kernel, patches, rows * patches),
        out_shape=[
            jax.ShapeDtypeStruct((blk_dev, blk, width), BF16),
            jax.ShapeDtypeStruct((rank, rows), F32),
        ],
        in_specs=[anywhere] * 5,
        out_specs=[anywhere, anywhere],
        scratch_shapes=[
            pltpu.VMEM(((2 * REACH + 1) * blk_dev + 1, blk, width), BF16),
            pltpu.VMEM(near_field.shape, BF16),
            pltpu.SMEM((blk_dev, slots), jnp.int32),
            pltpu.SMEM((blk_dev,), jnp.int32),
            pltpu.SMEM((blk_dev, slots), jnp.int32),
            pltpu.VMEM((width, sketch), BF16),
            pltpu.VMEM((4, rank, width), BF16),
            pltpu.VMEM((blk_dev, blk, width), BF16),
            pltpu.VMEM((CHUNKS, 2 * rank, cw), F32),
            pltpu.VMEM((CHUNKS, 2 * rank, cw), F32),
            pltpu.VMEM((CHUNKS, 2 * rank, cw), F32),
            pltpu.VMEM((CHUNKS, rank, cw), F32),
            pltpu.VMEM((CHUNKS, rank, cw), BF16),
            pltpu.VMEM((CHUNKS, rank, cw), BF16),
            pltpu.VMEM((CHUNKS, 3 * rank, cw), BF16),
            pltpu.VMEM((len(plan), rank // 2, 2 * rank), F32),
            pltpu.VMEM((sends, rank // 2, 2 * rank), F32),
            pltpu.VMEM((rank, rows), F32),
            dma((8,)), dma((8,)), dma((4,)), dma((CHUNKS,)), dma((CHUNKS,)),
            dma((CHUNKS,)), dma((CHUNKS,)), dma((CHUNKS,)), dma((CHUNKS,)),
            dma((sends,)), dma((sends,)), dma((CHUNKS,)),
        ],
        compiler_params=pltpu.CompilerParams(
            collective_id=0, has_side_effects=True, vmem_limit_bytes=64 * 2**20
        ),
    )(
        probe_columns.reshape(blk_dev, blk, width), near_field, column_ids, block_counts,
        sketch_matrix,
    )
    return (sample.reshape(rows, width), basis)


def solution(mesh):
    placed = (P("patch", "probe"), P("patch", None, None, None), P("patch", None), P("patch"), P())
    return jax.shard_map(
        shards,
        mesh=mesh,
        in_specs=placed,
        out_specs=(P("patch", "probe"), P("probe", "patch")),
        check_vma=False,
    )
```

```python
import functools
import math

import jax
import jax.numpy as jnp
from jax import lax
from jax.experimental import pallas as pl
from jax.experimental.pallas import tpu as pltpu
from jax.sharding import PartitionSpec as P

REACH = 2
MESH = pl.DeviceIdType.MESH
F32 = jnp.float32
BF16 = jnp.bfloat16
CHUNKS = 4
NT = (((1,), (1,)), ((), ()))
NN = (((1,), (0,)), ((), ()))
ROW_TILE = 8


def exchange_plan(patches):
    levels = patches.bit_length() - 1
    return [
        [digit << low for digit in range(1, 2 ** min(3, levels - low))]
        for low in range(0, levels, 3)
    ]


def eliminate(work, rank):
    tile = ROW_TILE
    shape = (tile, work.shape[1])
    tiles = [work[i : i + tile] for i in range(0, rank, tile)]
    row = lax.broadcasted_iota(jnp.int32, shape, 0)
    lane = lax.broadcasted_iota(jnp.int32, shape, 1)
    for t in range(len(tiles)):
        live = range(t, len(tiles))
        columns = [
            {i: jnp.broadcast_to(tiles[i][:, rank + t * tile + k : rank + t * tile + k + 1], shape) for i in live}
            for k in range(tile)
        ]
        for k in range(tile):
            scale = 1.0 / columns[k][t][k : k + 1, :]
            ratio = {i: columns[k][i] * scale for i in live}
            ratio[t] = jnp.where(row > k, ratio[t], 0.0)
            for later in columns[k + 1 :]:
                pivot = later[t][k : k + 1, :]
                for i in live:
                    later[i] = later[i] - ratio[i] * pivot
            pivot = tiles[t][k : k + 1, :]
            for i in live:
                tiles[i] = tiles[i] - ratio[i] * pivot
    diagonal = [
        jnp.sum(jnp.where(lane == row + rank + i * tile, part, 0.0), axis=1, keepdims=True)
        for i, part in enumerate(tiles)
    ]
    return jnp.concatenate(tiles, 0), jnp.concatenate(diagonal, 0)


def kernel(
    patches, probe, nf, ids_in, counts_in, psi, sample_out, split_out, packed_out,
    win, nfv, ids, counts, idx, psiv, psit, samp, keep, send, crecv, fac, xsend, xrecv, split, gsend, grecv,
    hs, hr, ls, nfs, sos, cs, cr, xs, xr, gs, gr, bos,
):
    blk_dev, slots, blk, width = nf.shape[0], nf.shape[1], nf.shape[2], probe.shape[2]
    half = blk_dev // 2
    sketch = psi.shape[1]
    rank = sketch // 4
    per = blk_dev // CHUNKS
    cw = per * blk
    levels = patches.bit_length() - 1

    p = lax.axis_index("patch")
    me = lax.axis_index("probe")
    s = 1 - 2 * (p % 2)
    near = p + s
    ahead = p + 2 * s
    behind = p - 2 * s
    has_ahead = jnp.logical_and(ahead >= 0, ahead < patches)
    has_behind = jnp.logical_and(behind >= 0, behind < patches)
    core = me + 1 - 2 * (me % 2)
    side = me + 2 - 4 * (me // 2)

    def other_patch(mask):
        place = p
        for bit in (2**level for level in range(levels)):
            if mask & bit:
                place = place + bit - 2 * bit * ((p // bit) % 2)
        return place

    peers = exchange_plan(patches)
    group = peers[0][-1] + 1

    barrier = pltpu.get_barrier_semaphore()

    def greet(where):
        pl.semaphore_signal(barrier, inc=1, device_id=where, device_id_type=MESH)

    ahead_out = jnp.logical_and(has_ahead, ahead // group != p // group)
    behind_out = jnp.logical_and(has_behind, behind // group != p // group)
    greet({"probe": core})
    greet({"probe": side})
    for stage in peers:
        for mask in stage:
            greet({"patch": other_patch(mask)})

    @pl.when(ahead_out)
    def _():
        greet({"patch": ahead})

    @pl.when(behind_out)
    def _():
        greet({"patch": behind})

    own_copy = pltpu.make_async_copy(probe, win.at[pl.ds(0, blk_dev)], ls.at[0])
    own_copy.start()
    psi_copy = pltpu.make_async_copy(
        psi.at[pl.ds(pl.multiple_of(me * width, width), width)], psiv, ls.at[1]
    )
    psi_copy.start()
    ids_copy = pltpu.make_async_copy(ids_in, ids, ls.at[2])
    ids_copy.start()
    counts_copy = pltpu.make_async_copy(counts_in, counts, ls.at[3])
    counts_copy.start()

    greeted = 2 + sum(len(stage) for stage in peers)
    pl.semaphore_wait(barrier, greeted + ahead_out.astype(jnp.int32) + behind_out.astype(jnp.int32))

    def halo(k, src, slot, start, count, target):
        return pltpu.make_async_remote_copy(
            src_ref=src, dst_ref=win.at[pl.ds(slot * blk_dev + start, count)],
            send_sem=hs.at[k], recv_sem=hr.at[k], device_id={"patch": target}, device_id_type=MESH,
        )

    first, second = probe.at[pl.ds(0, half)], probe.at[pl.ds(half, half)]
    near_b = halo(0, second, 1, half, half, near)
    near_a = halo(1, first, 1, 0, half, near)
    behind_a = halo(2, first, 2, 0, half, behind)
    behind_b = halo(3, second, 2, half, half, behind)
    ahead_a = halo(4, first, 3, 0, half, ahead)
    ahead_b = halo(5, second, 3, half, half, ahead)
    relay_a = halo(6, win.at[pl.ds(2 * blk_dev, half)], 4, 0, half, near)
    relay_b = halo(7, win.at[pl.ds(blk_dev + half, half)], 4, half, half, ahead)

    near_b.start()

    @pl.when(has_behind)
    def _():
        behind_a.start()

    @pl.when(has_ahead)
    def _():
        ahead_a.start()

    near_a.start()

    @pl.when(has_behind)
    def _():
        behind_b.start()

    @pl.when(has_ahead)
    def _():
        ahead_b.start()

    nf_copies = []
    for c in range(CHUNKS):
        rows = pl.ds(c * per, per)
        copy = pltpu.make_async_copy(nf.at[rows], nfv.at[rows], nfs.at[c])
        copy.start()
        nf_copies.append(copy)

    zero_block = (2 * REACH + 1) * blk_dev
    win[zero_block] = jnp.zeros((blk, width), BF16)

    ids_copy.wait()
    counts_copy.wait()

    @pl.loop(0, blk_dev)
    def _(b):
        live = counts[b]
        for n in range(slots):
            column = ids[b, n]
            turn = (column // blk_dev - p) * s
            slot = jnp.where(turn < 0, turn + 2 * REACH + 1, turn)
            place = slot * blk_dev + column % blk_dev
            idx[b, n] = jnp.where(n < live, place, zero_block)

    psi_copy.wait()
    psit[...] = psiv[...].astype(F32).T.astype(BF16).reshape(4, rank, width)
    other = side + 1 - 2 * (side % 2)
    psiq = jnp.concatenate([psit[me], psit[side], psit[core], psit[other]], 0)

    near_b.wait_recv()

    @pl.when(has_ahead)
    def _():
        relay_b.start()
        behind_a.wait_recv()
        relay_a.start()
        behind_b.wait_recv()

    near_a.wait_recv()

    @pl.when(has_behind)
    def _():
        ahead_a.wait_recv()
        ahead_b.wait_recv()
        relay_a.wait_recv()
        relay_b.wait_recv()

    own_copy.wait()

    def core_copy(c):
        return pltpu.make_async_remote_copy(
            src_ref=send.at[c], dst_ref=crecv.at[c], send_sem=cs.at[c], recv_sem=cr.at[c],
            device_id={"probe": core}, device_id_type=MESH,
        )

    def side_copy(c):
        return pltpu.make_async_remote_copy(
            src_ref=xsend.at[c], dst_ref=xrecv.at[c], send_sem=xs.at[c], recv_sem=xr.at[c],
            device_id={"probe": side}, device_id_type=MESH,
        )

    def pass_on(c):
        core_copy(c).wait_recv()
        both = keep[c] + crecv[c]
        fac[c] = both[:rank]
        xsend[c] = both[rank:].astype(BF16)
        side_copy(c).start()

    sample_copies = []
    for c in range(CHUNKS):
        nf_copies[c].wait()

        @pl.loop(c * per, (c + 1) * per)
        def _(b):
            picked = jnp.concatenate([win[idx[b, n]] for n in range(slots)], 0)
            blocks = jnp.concatenate([nfv[b, n] for n in range(slots)], 1)
            samp[b] = lax.dot_general(blocks, picked, NN, preferred_element_type=F32).astype(BF16)

        rows = pl.ds(c * per, per)
        copy = pltpu.make_async_copy(samp.at[rows], sample_out.at[rows], sos.at[c])
        copy.start()
        sample_copies.append(copy)
        part = lax.dot_general(
            psiq, samp[rows].reshape(cw, width), NT, preferred_element_type=F32
        )
        keep[c] = part[: 2 * rank]
        send[c] = part[2 * rank :]
        core_copy(c).start()
        if c > 0:
            pass_on(c - 1)
    pass_on(CHUNKS - 1)

    split_copies = []
    gram = jnp.zeros((rank, 2 * rank), F32)
    for c in range(CHUNKS):
        side_copy(c).wait_recv()
        factor = fac[c] + xrecv[c].astype(F32)
        high = factor.astype(BF16)
        low = (factor - high.astype(F32)).astype(BF16)
        split[c] = jnp.concatenate([high, low, high], 0)
        copy = pltpu.make_async_copy(split.at[c], split_out.at[c], bos.at[c])
        copy.start()
        split_copies.append(copy)
        twice_high = jnp.concatenate([high, high], 0)
        twice_low = jnp.concatenate([low, low], 0)
        both = lax.dot_general(split[c, : 2 * rank], twice_high, NT, preferred_element_type=F32)
        cross = lax.dot_general(high, twice_low, NT, preferred_element_type=F32)
        gram += both[:rank] + (both[rank:] + cross)

    lane = lax.broadcasted_iota(jnp.int32, (rank // 2, 2 * rank), 1)
    packed = jnp.where(lane < rank, gram[: rank // 2], gram[rank // 2 :])

    gram_copies = []
    place = 0
    for number, stage in enumerate(peers):
        gsend[number] = packed
        copies = []
        for mask in stage:
            copy = pltpu.make_async_remote_copy(
                src_ref=gsend.at[number], dst_ref=grecv.at[place], send_sem=gs.at[place],
                recv_sem=gr.at[place], device_id={"patch": other_patch(mask)}, device_id_type=MESH,
            )
            copy.start()
            copies.append((copy, place))
            place += 1
        for copy, slot in copies:
            copy.wait_recv()
            packed = packed + grecv[slot]
        gram_copies += copies

    packed_out[...] = packed

    near_b.wait_send()
    near_a.wait_send()

    @pl.when(has_behind)
    def _():
        behind_a.wait_send()
        behind_b.wait_send()

    @pl.when(has_ahead)
    def _():
        ahead_a.wait_send()
        ahead_b.wait_send()
        relay_a.wait_send()
        relay_b.wait_send()

    for c in range(CHUNKS):
        core_copy(c).wait_send()
        side_copy(c).wait_send()
        sample_copies[c].wait()
        split_copies[c].wait()
    for copy, _ in gram_copies:
        copy.wait_send()


def finish(total_rows, sample, split, packed, sample_out, basis_out, bas, ss, bs):
    rank, cw = 2 * packed.shape[0], split.shape[2]
    sample_copy = pltpu.make_async_copy(sample, sample_out, ss.at[0])
    sample_copy.start()
    lane = lax.broadcasted_iota(jnp.int32, (rank, 2 * rank), 1)
    row = lax.broadcasted_iota(jnp.int32, (rank, 2 * rank), 0)
    work = jnp.concatenate([pltpu.roll(packed[...], rank, 1), packed[...]], 0)
    work = jnp.where(lane < rank, jnp.where(lane == row, 1.0, 0.0), work)
    work, pivots = eliminate(work, rank)
    inverse = work[:, :rank] * (lax.rsqrt(pivots) * math.sqrt(total_rows))
    inverse_high = inverse.astype(BF16)
    inverse_low = (inverse - inverse_high.astype(F32)).astype(BF16)
    inverse = jnp.concatenate([inverse_high, inverse_high, inverse_low], 1)

    basis_copies = []
    for c in range(CHUNKS):
        columns = pl.ds(c * cw, cw)
        bas[:, columns] = lax.dot_general(
            inverse, split[c], NN, preferred_element_type=F32
        )
        copy = pltpu.make_async_copy(bas.at[:, columns], basis_out.at[:, columns], bs.at[c])
        copy.start()
        basis_copies.append(copy)
    for copy in basis_copies:
        copy.wait()
    sample_copy.wait()


def shards(probe_columns, near_field, column_ids, block_counts, sketch_matrix):
    blk_dev, slots, blk, _ = near_field.shape
    rows, width = probe_columns.shape
    sketch = sketch_matrix.shape[1]
    patches = lax.axis_size("patch")
    rank = sketch // lax.axis_size("probe")
    cw = rows // CHUNKS
    plan = exchange_plan(patches)
    sends = sum(len(stage) for stage in plan)
    anywhere = pl.BlockSpec(memory_space=pltpu.HBM)
    dma = pltpu.SemaphoreType.DMA
    operands = (
        probe_columns.reshape(blk_dev, blk, width), near_field, column_ids, block_counts, sketch_matrix
    )
    in_hbm = [pltpu.with_memory_space_constraint(operand, pltpu.HBM) for operand in operands]
    held = pl.BlockSpec(memory_space=pltpu.VMEM)
    sample, split, packed = pl.pallas_call(
        functools.partial(kernel, patches),
        out_shape=[
            jax.ShapeDtypeStruct((blk_dev, blk, width), BF16),
            jax.ShapeDtypeStruct((CHUNKS, 3 * rank, cw), BF16),
            jax.ShapeDtypeStruct((rank // 2, 2 * rank), F32),
        ],
        in_specs=[anywhere] * 5,
        out_specs=[anywhere, anywhere, held],
        scratch_shapes=[
            pltpu.VMEM(((2 * REACH + 1) * blk_dev + 1, blk, width), BF16),
            pltpu.VMEM(near_field.shape, BF16),
            pltpu.SMEM((blk_dev, slots), jnp.int32),
            pltpu.SMEM((blk_dev,), jnp.int32),
            pltpu.SMEM((blk_dev, slots), jnp.int32),
            pltpu.VMEM((width, sketch), BF16),
            pltpu.VMEM((4, rank, width), BF16),
            pltpu.VMEM((blk_dev, blk, width), BF16),
            pltpu.VMEM((CHUNKS, 2 * rank, cw), F32),
            pltpu.VMEM((CHUNKS, 2 * rank, cw), F32),
            pltpu.VMEM((CHUNKS, 2 * rank, cw), F32),
            pltpu.VMEM((CHUNKS, rank, cw), F32),
            pltpu.VMEM((CHUNKS, rank, cw), BF16),
            pltpu.VMEM((CHUNKS, rank, cw), BF16),
            pltpu.VMEM((CHUNKS, 3 * rank, cw), BF16),
            pltpu.VMEM((len(plan), rank // 2, 2 * rank), F32),
            pltpu.VMEM((sends, rank // 2, 2 * rank), F32),
            dma((8,)), dma((8,)), dma((4,)), dma((CHUNKS,)), dma((CHUNKS,)),
            dma((CHUNKS,)), dma((CHUNKS,)), dma((CHUNKS,)), dma((CHUNKS,)),
            dma((sends,)), dma((sends,)), dma((CHUNKS,)),
        ],
        compiler_params=pltpu.CompilerParams(
            collective_id=0, has_side_effects=True, vmem_limit_bytes=48 * 2**20
        ),
    )(*in_hbm)
    sample, basis = pl.pallas_call(
        functools.partial(finish, rows * patches),
        out_shape=[
            jax.ShapeDtypeStruct((blk_dev, blk, width), BF16),
            jax.ShapeDtypeStruct((rank, rows), F32),
        ],
        in_specs=[anywhere, held, held],
        out_specs=[anywhere, anywhere],
        scratch_shapes=[pltpu.VMEM((rank, rows), F32), dma((1,)), dma((CHUNKS,))],
        compiler_params=pltpu.CompilerParams(vmem_limit_bytes=16 * 2**20),
    )(sample, split, packed)
    return (sample.reshape(rows, width), basis)


def solution(mesh):
    placed = (P("patch", "probe"), P("patch", None, None, None), P("patch", None), P("patch"), P())
    return jax.shard_map(
        shards,
        mesh=mesh,
        in_specs=placed,
        out_specs=(P("patch", "probe"), P("probe", "patch")),
        check_vma=False,
    )
```
